32 devices in a mesh: fsdp: 2 (over core), expert: 16 (over z, y, x).
Axes of the slice: x: 2, y: 2, z: 4, core: 2. Of those that a mesh axis runs over, the one named last changes fastest.
Arguments:
- tokens: bfloat16 [3, 256, 7168], P(None, 'expert'), may hold values from -6 to 6
- route_ids: int32 [3, 256, 8], P(None, 'expert'), may hold values from 0 to 15, all different within a row; in each aligned block of 16 rows (0 to 15, 16 to 31, ..., all dimensions but the last counted through in order) at most 12 rows name the same one
- gate_values: bfloat16 [3, 256, 8], P(None, 'expert'), may hold values from 0.25 to 1
- cap_limit: int32 [16], replicated, may hold values from 6 to 12
- update_ids: int32 [16], replicated, may hold values from 0 to 15, each once
- expert_weights: bfloat16 [16, 7168, 3072], P(None, ('fsdp', 'expert')), may hold values from -0.109375 to 0.109375
Outputs:
- moe_output: bfloat16 [3, 256, 7168], P(None, 'expert', 'fsdp')
The draws below stay inside these ranges and needn't reach their ends.
Inputs may be any that keep to these rules, and one draw needn't show every extreme that they name: `route_ids`: each row names 8 different experts. In every aligned block of 16 rows of one step (the rows of one device) no expert is named by more than 12 rows, a bound that some block reaches. `update_ids`: each expert once.
All inputs are finite; a program needn't handle non-finite values.
Results may differ from the reference program's by a relative error of at most 0.0058.
Values may be sent and summed in bfloat16 or wider, within the bound.
A program may use at most 192 MiB of HBM per device.

```python
import math
import jax
import jax.numpy as jnp
import numpy as np
from jax import lax

D = 7168
H = 1024
TOP = 8
STEPS = 3
ROWS_DEV = 16
EXPERTS = 16
ROWS = 256
CAP = 12
N_EXPERT = 16


def draw_cap_limit(key, part):
    first_key = jax.random.fold_in(key, 11)
    second_key = jax.random.fold_in(key, 23)
    reduction = jax.random.randint(first_key, (EXPERTS,), 0, CAP // 2 + 1)
    chosen = jax.random.randint(second_key, (), 0, EXPERTS)
    index_row = jnp.arange(EXPERTS, dtype=jnp.int32)
    reduction = jnp.where(index_row == chosen, 0, reduction)
    reduction = jnp.where(index_row == (chosen + 1) % EXPERTS, CAP // 2, reduction)
    return (CAP - reduction).astype(jnp.int32)


def level_of(rng, shape, split, least, top_value):
    def one(axis_at, parts):
        draws = jax.random.uniform(jax.random.fold_in(jax.random.fold_in(rng, 6), axis_at), (parts,), jnp.float32, least / len(split), top_value / len(split))
        return jnp.repeat(jnp.exp(draws), shape[axis_at] // parts).reshape((-1,) + (1,) * (len(shape) - axis_at - 1))

    gain = one(*split[0])
    for cut in split[1:]:
        gain = gain * one(*cut)
    return gain


def assign_block(own_key, own, number, rows, amount, top, limit, lean):
    order = jax.random.permutation(own_key, amount)
    packed, common = portions_of(amount, rows * top, limit, lean, True), portions_of(amount, rows * top, limit, lean, False)
    places = jnp.arange(amount)

    def named(sizes, turn):
        used = int((sizes > 0).sum())
        fixed = max(1, used // 4)
        shifted = fixed + (places - fixed + turn * (used - fixed)) % max(1, amount - fixed)
        return jnp.zeros((amount,), jnp.int32).at[order[jnp.where(places < fixed, places, shifted)]].set(jnp.asarray(sizes, jnp.int32))

    sizes = jnp.where(number % 4 == 0, named(packed, number // 4), named(common, number - number // 4 - 1))
    mixed = jax.random.permutation(jax.random.fold_in(own, 3), amount)
    source_of, receiver = mixed[0:amount // 2 * 2:2], mixed[1:amount // 2 * 2:2]
    slack = jnp.minimum(sizes[source_of] - 1, limit - sizes[receiver]) // 2
    slack = jnp.where((source_of == order[0]) | (receiver == order[0]) | (sizes[receiver] == 0), 0, jnp.maximum(slack, 0))
    shifted = jax.random.randint(jax.random.fold_in(own, 4), (amount // 2,), 0, 1 << 20) % (slack + 1)
    sizes = sizes.at[source_of].add(-shifted).at[receiver].add(shifted)
    labels = jnp.searchsorted(jnp.cumsum(sizes), jnp.arange(rows * top), side="right").astype(jnp.int32)
    grid = labels.reshape(top, rows).T
    grid = grid[jax.random.permutation(jax.random.fold_in(own, 1), rows)]
    turn = jax.random.randint(jax.random.fold_in(own, 2), (rows, 1), 0, top)
    return jnp.take_along_axis(grid, (jnp.arange(top)[None, :] + turn) % top, axis=1)


def portions_of(amount, total, most, skew, full):
    loads = [(1 << 20) // math.isqrt(standing ** skew) + 1 for standing in range(1, amount + 1)]
    largest = most if full else min(most, max(-(-total // amount), total * loads[0] // sum(loads)))
    least = 1 if total - largest >= amount - 1 else 0
    holding, spare = [largest] + [least] * (amount - 1), total - largest - least * (amount - 1)
    while spare > 0:
        candidates = [i for i in range(1, amount) if holding[i] < largest] or [i for i in range(1, amount) if holding[i] < most]
        pool, budget = sum([loads[i] for i in candidates]), spare
        for i in candidates:
            addition = min(most - holding[i], max(1, budget * loads[i] // pool), spare)
            holding[i] = holding[i] + addition
            spare = spare - addition
    return np.array(holding)


def noise(key, shape, scale, bound, pieces=(), kind=jnp.bfloat16):
    values = jax.random.normal(key, shape, jnp.float32) * scale
    if len(pieces) > 0:
        values = level_of(key, shape, pieces, -0.22, 0.18) * values
    return jnp.clip(values, min=-bound, max=bound).astype(kind)


def setup_inputs(seed: int = 0) -> dict:
    key_of = jax.random.split(jax.random.key(seed), 7)
    tokens = noise(key_of[0], (STEPS, ROWS, D), 1.0, 6.0, ((1, 16),))
    route_ids_keys = jax.random.split(jax.random.fold_in(key_of[1], 1), STEPS * ROWS // ROWS_DEV)
    route_ids_turns = jax.random.permutation(jax.random.fold_in(key_of[1], 3), STEPS * ROWS // ROWS_DEV)
    route_ids = jax.vmap(lambda own, number: assign_block(jax.random.fold_in(key_of[1], 2), own, number, ROWS_DEV, EXPERTS, TOP, CAP, 2))(route_ids_keys, route_ids_turns).reshape((STEPS, ROWS, TOP))
    gate_values = jnp.clip(0.25 + 0.75 * jax.random.uniform(key_of[2], (STEPS, ROWS, TOP), jnp.float32) ** level_of(key_of[2], (STEPS, ROWS, TOP), ((1, 16),), -0.2, 0.2), 0.25, 1.0).astype(jnp.bfloat16)
    cap_limit = draw_cap_limit(jax.random.fold_in(key_of[6], 71), 0)
    update_ids = jax.random.permutation(key_of[4], EXPERTS).astype(jnp.int32)
    expert_weights = noise(key_of[5], (EXPERTS, D, 3 * H), (3 * H) ** -0.5, 0.109375, ((1, 32),))
    return {"tokens": tokens, "route_ids": route_ids, "gate_values": gate_values, "cap_limit": cap_limit, "update_ids": update_ids, "expert_weights": expert_weights}


def ffn_rows(rows_in, weights, hidden_all):
    gate_part = jnp.dot(rows_in, weights[:, :hidden_all], preferred_element_type=jnp.float32)
    up_part = jnp.dot(rows_in, weights[:, hidden_all:2 * hidden_all], preferred_element_type=jnp.float32)
    hidden = (jax.nn.silu(gate_part) * up_part).astype(jnp.bfloat16)
    return lax.dot_general(hidden, weights[:, 2 * hidden_all:], (((1,), (1,)), ((), ())), preferred_element_type=jnp.float32).astype(jnp.bfloat16)


def reference(tokens, route_ids, gate_values, cap_limit, update_ids, expert_weights):
    inverse_order = jnp.argsort(update_ids).astype(jnp.int32)
    ordered = jnp.take(expert_weights, inverse_order, axis=0)
    blocks = N_EXPERT
    per_block = ROWS_DEV * TOP
    total_slots = blocks * CAP
    outputs = []
    for step_index in range(STEPS):
        ids_block = route_ids[step_index].reshape(blocks, per_block).astype(jnp.int32)
        expert_hot = (ids_block[:, :, None] == jnp.arange(EXPERTS, dtype=jnp.int32)[None, None, :]).astype(jnp.int32)
        position = jnp.sum((jnp.cumsum(expert_hot, axis=1) - 1) * expert_hot, axis=2).astype(jnp.int32)
        limit_row = jnp.take(cap_limit, ids_block, axis=0)
        kept_mask = position < limit_row
        block_index = jnp.arange(blocks, dtype=jnp.int32)[:, None]
        global_slot = ids_block * total_slots + block_index * CAP + position
        row_global = block_index * ROWS_DEV + jnp.arange(per_block, dtype=jnp.int32)[None, :] // TOP
        target = jnp.where(kept_mask, global_slot, EXPERTS * total_slots).astype(jnp.int32)
        source_row = jnp.full((EXPERTS * total_slots,), ROWS, jnp.int32).at[target.reshape(-1)].set(row_global.reshape(-1).astype(jnp.int32), mode="drop")
        padded_tokens = jnp.concatenate([tokens[step_index], jnp.zeros((1, D), jnp.bfloat16)], axis=0)
        gathered = jnp.take(padded_tokens, source_row, axis=0).reshape(EXPERTS, total_slots, D)
        expert_out = lax.map(lambda operands: ffn_rows(operands[0], operands[1], H), (gathered, ordered))
        flat_out = jnp.concatenate([expert_out.reshape(EXPERTS * total_slots, D), jnp.zeros((1, D), jnp.bfloat16)], axis=0)
        picked = jnp.take(flat_out, target.reshape(-1), axis=0).astype(jnp.float32)
        weight_flat = gate_values[step_index].reshape(-1).astype(jnp.float32)
        mixed_rows = jnp.sum((picked * weight_flat[:, None]).reshape(ROWS, TOP, D), axis=1)
        outputs.append(mixed_rows.astype(jnp.bfloat16))
    return jnp.stack(outputs)
```

```python
import functools

import jax
import jax.numpy as jnp
from jax import lax
from jax.experimental import pallas as pl
from jax.experimental.pallas import tpu as pltpu
from jax.sharding import PartitionSpec as P

TILE = 128
ALIGN = 16
BF16 = jnp.bfloat16
F32 = jnp.float32


def dot(a, b, ca=1, cb=0):
    return lax.dot_general(a, b, (((ca,), (cb,)), ((), ())), preferred_element_type=F32)


def tables(route_ids, gate_values, cap_limit, block_rows):
    rows = route_ids.shape[0]
    experts = cap_limit.shape[0]
    hot = route_ids[:, :, None] == jnp.arange(experts, dtype=jnp.int32)[None, None, :]
    chosen = jnp.any(hot, axis=1)
    gates = jnp.sum(jnp.where(hot, gate_values[:, :, None].astype(F32), 0.0), axis=1)
    at = jnp.arange(rows, dtype=jnp.int32)
    earlier = at[None, :] < at[:, None]
    same = at[None, :] // block_rows == at[:, None] // block_rows
    position = dot((earlier & same).astype(BF16), chosen.astype(BF16)).astype(jnp.int32)
    kept = chosen & (position < cap_limit[None, :])
    before = dot(earlier.astype(BF16), kept.astype(BF16)).astype(jnp.int32)
    counts = jnp.sum(kept.astype(jnp.int32), axis=0)
    padded = (counts + (ALIGN - 1)) // ALIGN * ALIGN
    es = jnp.arange(experts, dtype=jnp.int32)
    starts = jnp.sum(jnp.where(es[None, :] < es[:, None], padded[None, :], 0), axis=1)
    slots = jnp.where(kept, before + starts[None, :], -1)
    chunks = (counts + (TILE - 1)) // TILE
    return slots.T[:, None, :], gates.T[:, None, :], starts, chunks


def up_kernel(parts, starts, chunks, order, mine, slots_ref, x_ref, *refs):
    weights, out_ref = refs[:-1], refs[-1]
    e = pl.program_id(0)
    local = x_ref.shape[2]

    @pl.when(e == 0)
    def _():
        out_ref[...] = jnp.zeros_like(out_ref)

    slots = slots_ref[0]

    def step(c, carry):
        base = pl.multiple_of(starts[e] + c * TILE, ALIGN)
        pick = slots == base + lax.broadcasted_iota(jnp.int32, (TILE, slots.shape[1]), 0)
        pick = pick.astype(F32).astype(BF16)
        a = b = None
        for i in range(parts):
            xs = dot(pick, x_ref[i]).astype(BF16)
            da = dot(xs, weights[2 * i][0])
            db = dot(xs, weights[2 * i + 1][0])
            a, b = (da, db) if a is None else (a + da, b + db)
        out_ref[0, pl.ds(base, TILE), :] = a.astype(out_ref.dtype)
        out_ref[1, pl.ds(base, TILE), :] = b.astype(out_ref.dtype)
        return carry

    lax.fori_loop(0, chunks[e], step, 0)


def down_kernel(parts, starts, chunks, order, mine, slots_ref, gates_ref, h_ref, *refs):
    weights, out_ref = refs[:-1], refs[-1]
    e = pl.program_id(0)
    total = h_ref.shape[0]

    @pl.when(e == 0)
    def _():
        out_ref[...] = jnp.zeros_like(out_ref)

    slots = slots_ref[0]
    gates = gates_ref[0]

    def step(c, carry):
        first = starts[e] + c * TILE
        base = pl.multiple_of(jnp.minimum(first, total - TILE), ALIGN)
        number = base + lax.broadcasted_iota(jnp.int32, (TILE, slots.shape[1]), 0)
        mix = jnp.where((slots == number) & (number >= first), gates, 0.0).astype(BF16)
        h = h_ref[pl.ds(base, TILE), :]
        for i in range(parts):
            y = dot(h, weights[i][0], 1, 1)
            high = y.astype(BF16)
            low = (y - high.astype(F32)).astype(BF16)
            out_ref[i] += dot(mix, high, 0, 0) + dot(mix, low, 0, 0)
        return carry

    lax.fori_loop(0, chunks[e], step, 0)


def halving(part, order):
    n = part.shape[0]
    bits = n.bit_length() - 1
    me = lax.axis_index("expert")
    cur = part.reshape((2,) * bits + part.shape[1:])
    left = list(range(bits - 1, -1, -1))
    for b in order:
        axis = left.index(b)
        bit = (me >> b) & 1
        send = lax.dynamic_index_in_dim(cur, 1 - bit, axis, keepdims=False).astype(BF16)
        keep = lax.dynamic_index_in_dim(cur, bit, axis, keepdims=False).astype(F32)
        got = lax.ppermute(send, "expert", [(i, i ^ (1 << b)) for i in range(n)])
        cur = keep + got.astype(F32)
        left.pop(axis)
    return cur


def body(tokens, route_ids, gate_values, cap_limit, update_ids, expert_weights):
    steps, block_rows, width = tokens.shape
    top = route_ids.shape[2]
    experts = cap_limit.shape[0]
    parts = lax.axis_size("fsdp")
    owners = lax.axis_size("expert")
    local = expert_weights.shape[1]
    hidden = expert_weights.shape[2] // 3
    share = hidden // parts
    rows = steps * owners * block_rows
    f = lax.axis_index("fsdp")

    es = jnp.arange(experts, dtype=jnp.int32)
    order = jnp.sum(jnp.where(update_ids[None, :] == es[:, None], es[None, :], 0), axis=1)
    ids = lax.all_gather(route_ids, "expert", axis=1, tiled=True).reshape(rows, top)
    gate = lax.all_gather(gate_values, "expert", axis=1, tiled=True).reshape(rows, top)
    slots, gates, starts, chunks = tables(ids, gate, cap_limit, block_rows)

    x = tokens.reshape(steps, block_rows, parts, owners, local)
    x = jnp.transpose(x, (3, 2, 0, 1, 4))
    x = lax.all_to_all(x, "expert", split_axis=0, concat_axis=0, tiled=True)
    x = jnp.transpose(x, (1, 2, 0, 3, 4)).reshape(parts, rows, local)

    others = []
    for s in range(1, parts):
        to = (f + s) % parts
        cut = expert_weights.reshape(experts, local, 3, parts, share)
        cut = lax.dynamic_index_in_dim(cut, to, 3, keepdims=False)
        cut = jnp.transpose(cut, (2, 0, 1, 3))
        others.append(lax.ppermute(cut, "fsdp", [(i, (i + s) % parts) for i in range(parts)]))
    sources = [(f - s) % parts for s in range(parts)]
    x = jnp.stack([lax.dynamic_index_in_dim(x, i, 0, keepdims=False) for i in sources])

    packed = -(-(rows * top + experts * (ALIGN - 1)) // (ALIGN * owners)) * ALIGN * owners
    mine = f.astype(jnp.int32).reshape(1)
    whole = lambda *shape: pl.BlockSpec(shape, lambda e, *_: (0,) * len(shape))
    line = pl.BlockSpec((1, 1, rows), lambda e, *_: (e, 0, 0))

    def own(kind):
        return pl.BlockSpec((1, local, share), lambda e, st, ch, od, mi: (od[e], 0, kind * parts + mi[0]))

    def other(kind):
        return pl.BlockSpec((None, 1, local, share), lambda e, st, ch, od, mi: (kind, od[e], 0, 0))

    scalars = (starts, chunks, order, mine)
    params = pltpu.CompilerParams(vmem_limit_bytes=58 * 2**20)
    up_specs, up_args, down_specs, down_args = [own(0), own(1)], [expert_weights] * 2, [own(2)], [expert_weights]
    for got in others:
        up_specs += [other(0), other(1)]
        up_args += [got, got]
        down_specs.append(other(2))
        down_args.append(got)

    ab = pl.pallas_call(
        functools.partial(up_kernel, parts),
        out_shape=jax.ShapeDtypeStruct((2, packed + TILE, share), BF16),
        grid_spec=pltpu.PrefetchScalarGridSpec(
            num_scalar_prefetch=4,
            grid=(experts,),
            in_specs=[line, whole(parts, rows, local)] + up_specs,
            out_specs=whole(2, packed + TILE, share),
        ),
        compiler_params=params,
        cost_estimate=pl.CostEstimate(flops=2 * packed * local * parts * 2 * share, bytes_accessed=3 * 10**7, transcendentals=0),
    )(*scalars, slots, x, *up_args)

    bits = owners.bit_length() - 1
    down_order = list(range(2, bits))[::-1]
    a = halving(ab[0, :packed].reshape(owners, packed // owners, share), [0, 1] + down_order)
    b = halving(ab[1, :packed].reshape(owners, packed // owners, share), [1, 0] + down_order)
    h = (a * jax.nn.sigmoid(a) * b).astype(BF16)
    h = lax.all_gather(h, "expert", axis=0, tiled=True)

    out = pl.pallas_call(
        functools.partial(down_kernel, parts),
        out_shape=jax.ShapeDtypeStruct((parts, rows, local), F32),
        grid_spec=pltpu.PrefetchScalarGridSpec(
            num_scalar_prefetch=4,
            grid=(experts,),
            in_specs=[line, line, whole(packed, share)] + down_specs,
            out_specs=whole(parts, rows, local),
        ),
        compiler_params=params,
        cost_estimate=pl.CostEstimate(flops=2 * packed * local * parts * (share + 2 * rows), bytes_accessed=2 * 10**7, transcendentals=0),
    )(*scalars, slots, gates, h, *down_args)

    total = lax.dynamic_index_in_dim(out, 0, 0, keepdims=False)
    for s in range(1, parts):
        total = total + lax.ppermute(out[s], "fsdp", [(i, (i - s) % parts) for i in range(parts)])
    y = total.astype(BF16).reshape(steps, owners, block_rows, local)
    y = lax.all_to_all(y, "expert", split_axis=1, concat_axis=1, tiled=True)
    return jnp.transpose(y, (0, 2, 1, 3)).reshape(steps, block_rows, owners * local)


def solution(mesh):
    return jax.shard_map(
        body,
        mesh=mesh,
        in_specs=(
            P(None, "expert", None),
            P(None, "expert", None),
            P(None, "expert", None),
            P(),
            P(),
            P(None, ("fsdp", "expert"), None),
        ),
        out_specs=P(None, "expert", "fsdp"),
        check_vma=False,
    )
```

```python
import functools

import jax
import jax.numpy as jnp
from jax import lax
from jax.experimental import pallas as pl
from jax.experimental.pallas import tpu as pltpu
from jax.sharding import PartitionSpec as P

TILE = 128
HALVES = 2
ALIGN = 16
BF16 = jnp.bfloat16
F32 = jnp.float32


def dot(a, b, ca=1, cb=0):
    return lax.dot_general(a, b, (((ca,), (cb,)), ((), ())), preferred_element_type=F32)


def tables(route_ids, gate_values, cap_limit, block_rows):
    rows = route_ids.shape[0]
    experts = cap_limit.shape[0]
    hot = route_ids[:, :, None] == jnp.arange(experts, dtype=jnp.int32)[None, None, :]
    chosen = jnp.any(hot, axis=1)
    gates = jnp.sum(jnp.where(hot, gate_values[:, :, None].astype(F32), 0.0), axis=1)
    at = jnp.arange(rows, dtype=jnp.int32)
    earlier = at[None, :] < at[:, None]
    same = at[None, :] // block_rows == at[:, None] // block_rows
    position = dot((earlier & same).astype(BF16), chosen.astype(BF16)).astype(jnp.int32)
    kept = chosen & (position < cap_limit[None, :])
    before = dot(earlier.astype(BF16), kept.astype(BF16)).astype(jnp.int32)
    counts = jnp.sum(kept.astype(jnp.int32), axis=0)
    padded = (counts + (ALIGN - 1)) // ALIGN * ALIGN
    es = jnp.arange(experts, dtype=jnp.int32)
    starts = jnp.sum(jnp.where(es[None, :] < es[:, None], padded[None, :], 0), axis=1)
    slots = jnp.where(kept, before + starts[None, :], -1)
    chunks = (counts + (TILE - 1)) // TILE
    return slots.T[:, None, :], gates.T[:, None, :], starts, chunks


def up_kernel(parts, fresh, starts, chunks, order, mine, *refs):
    if fresh:
        slots_ref, x_ref, weights, (out_ref, packed_ref) = refs[0], refs[1], refs[2:-2], refs[-2:]
    else:
        packed_ref, weights, out_ref = refs[0], refs[1:-1], refs[-1]
    e = pl.program_id(0)

    @pl.when(e == 0)
    def _():
        out_ref[...] = jnp.zeros_like(out_ref)

    def step(c, carry):
        base = pl.multiple_of(starts[e] + c * TILE, ALIGN)
        if fresh:
            slots = slots_ref[0]
            pick = slots == base + lax.broadcasted_iota(jnp.int32, (TILE, slots.shape[1]), 0)
            pick = pick.astype(F32).astype(BF16)
        a = b = None
        for i in range(parts):
            if fresh:
                xs = dot(pick, x_ref[i]).astype(BF16)
                packed_ref[i, pl.ds(base, TILE), :] = xs
            else:
                xs = packed_ref[i, pl.ds(base, TILE), :]
            da = dot(xs, weights[2 * i][0])
            db = dot(xs, weights[2 * i + 1][0])
            a, b = (da, db) if a is None else (a + da, b + db)
        out_ref[0, pl.ds(base, TILE), :] = a.astype(out_ref.dtype)
        out_ref[1, pl.ds(base, TILE), :] = b.astype(out_ref.dtype)
        return carry

    lax.fori_loop(0, chunks[e], step, 0)


def down_kernel(parts, starts, chunks, order, mine, slots_ref, gates_ref, *refs):
    h_refs, weights, out_ref = refs[:HALVES], refs[HALVES:-1], refs[-1]
    e = pl.program_id(0)
    total, cols = h_refs[0].shape

    @pl.when(e == 0)
    def _():
        out_ref[...] = jnp.zeros_like(out_ref)

    slots = slots_ref[0]
    gates = gates_ref[0]

    def step(c, carry):
        first = starts[e] + c * TILE
        base = pl.multiple_of(jnp.minimum(first, total - TILE), ALIGN)
        number = base + lax.broadcasted_iota(jnp.int32, (TILE, slots.shape[1]), 0)
        mix = jnp.where((slots == number) & (number >= first), gates, 0.0).astype(BF16)
        h = [h_ref[pl.ds(base, TILE), :] for h_ref in h_refs]
        for i in range(parts):
            y = sum(dot(h[q], weights[i][0, :, q * cols : (q + 1) * cols], 1, 1) for q in range(HALVES))
            high = y.astype(BF16)
            low = (y - high.astype(F32)).astype(BF16)
            out_ref[i] += dot(mix, high, 0, 0) + dot(mix, low, 0, 0)
        return carry

    lax.fori_loop(0, chunks[e], step, 0)


def halve(cur, left, b, n):
    axis = left.index(b)
    bit = (lax.axis_index("expert") >> b) & 1
    send = lax.dynamic_index_in_dim(cur, 1 - bit, axis, keepdims=False).astype(BF16)
    keep = lax.dynamic_index_in_dim(cur, bit, axis, keepdims=False).astype(F32)
    got = lax.ppermute(send, "expert", [(i, i ^ (1 << b)) for i in range(n)])
    return keep + got.astype(F32), [i for i in left if i != b]


def reduce_all(pieces, n):
    bits = n.bit_length() - 1
    later = list(range(bits - 1, 1, -1))
    orders = ([0, 1] + later, [1, 0] + later)
    left = list(range(bits - 1, -1, -1))
    state = [[(i.reshape((2,) * bits + (i.shape[0] // n, i.shape[1])), left) for i in pair] for pair in pieces]
    done = [None] * len(state)
    for turn in range(bits + 2 * (len(state) - 1)):
        for q in range(len(state)):
            at = turn - 2 * q
            if 0 <= at < bits:
                state[q] = [halve(*state[q][k], orders[k][at], n) for k in range(2)]
        held = lax.optimization_barrier([[i for i, _ in pair] for pair in state])
        state = [[(i, pair[k][1]) for k, i in enumerate(new)] for new, pair in zip(held, state)]
        for q in range(len(state)):
            if turn - 2 * q == bits - 1:
                a, b = (i for i, _ in state[q])
                done[q] = lax.all_gather((a * jax.nn.sigmoid(a) * b).astype(BF16), "expert", axis=0, tiled=True)
    return done


def body(tokens, route_ids, gate_values, cap_limit, update_ids, expert_weights):
    steps, block_rows, width = tokens.shape
    top = route_ids.shape[2]
    experts = cap_limit.shape[0]
    parts = lax.axis_size("fsdp")
    owners = lax.axis_size("expert")
    local = expert_weights.shape[1]
    hidden = expert_weights.shape[2] // 3
    share = hidden // parts
    rows = steps * owners * block_rows
    f = lax.axis_index("fsdp")

    es = jnp.arange(experts, dtype=jnp.int32)
    order = jnp.sum(jnp.where(update_ids[None, :] == es[:, None], es[None, :], 0), axis=1)

    others = []
    for s in range(1, parts):
        to = (f + s) % parts
        pairs = [(i, (i + s) % parts) for i in range(parts)]
        cuts = [
            lax.dynamic_slice(expert_weights, (0, 0, kind * hidden + to * share), (experts, local, share))
            for kind in range(3)
        ]
        others.append([lax.ppermute(cut, "fsdp", pairs) for cut in cuts])

    x = tokens.reshape(steps, block_rows, parts, owners, local)
    x = jnp.transpose(x, (3, 0, 1, 2, 4)).reshape(owners, steps, block_rows, parts * local)
    routes = jnp.concatenate([route_ids.astype(BF16), gate_values], axis=2)
    routes = jnp.broadcast_to(routes[None], (owners,) + routes.shape)
    x = jnp.concatenate([x, routes], axis=3)
    x = lax.all_to_all(x, "expert", split_axis=0, concat_axis=0, tiled=True)
    x = jnp.transpose(x, (1, 0, 2, 3)).reshape(rows, parts * local + 2 * top)
    ids = x[:, parts * local : parts * local + top].astype(jnp.int32)
    gate = x[:, parts * local + top :]
    slots, gates, starts, chunks = tables(ids, gate, cap_limit, block_rows)
    sources = [(f - s) % parts for s in range(parts)]
    x = jnp.stack([lax.dynamic_slice(x, (0, i * local), (rows, local)) for i in sources])

    packed = -(-(rows * top + experts * (ALIGN - 1)) // (ALIGN * owners)) * ALIGN * owners
    mine = f.astype(jnp.int32).reshape(1)
    whole = lambda *shape: pl.BlockSpec(shape, lambda e, *_: (0,) * len(shape))
    line = pl.BlockSpec((1, 1, rows), lambda e, *_: (e, 0, 0))

    def own(kind, cols, q):
        return pl.BlockSpec((1, local, cols), lambda e, st, ch, od, mi: (od[e], 0, (kind * parts + mi[0]) * (share // cols) + q))

    def other(cols, q):
        return pl.BlockSpec((1, local, cols), lambda e, st, ch, od, mi: (od[e], 0, q))

    scalars = (starts, chunks, order, mine)
    params = pltpu.CompilerParams(vmem_limit_bytes=58 * 2**20)
    cols = share // HALVES
    xs = None
    pieces = []
    for q in range(HALVES):
        specs, args = [own(0, cols, q), own(1, cols, q)], [expert_weights] * 2
        for got in others:
            specs += [other(cols, q)] * 2
            args += got[:2]
        ab_shape = (2, packed + TILE, cols)
        xs_shape = (parts, packed + TILE, local)
        fresh = q == 0
        made = pl.pallas_call(
            functools.partial(up_kernel, parts, fresh),
            out_shape=[jax.ShapeDtypeStruct(i, BF16) for i in ([ab_shape, xs_shape] if fresh else [ab_shape])],
            grid_spec=pltpu.PrefetchScalarGridSpec(
                num_scalar_prefetch=4,
                grid=(experts,),
                in_specs=([line, whole(parts, rows, local)] if fresh else [whole(*xs_shape)]) + specs,
                out_specs=[whole(*i) for i in ([ab_shape, xs_shape] if fresh else [ab_shape])],
            ),
            compiler_params=params,
            cost_estimate=pl.CostEstimate(flops=2 * 10**10, bytes_accessed=5 * 10**7, transcendentals=0),
        )(*scalars, *([slots, x] if fresh else [xs]), *args)
        if fresh:
            xs = made[1]
        ab = made[0]
        pieces.append([ab[0, :packed], ab[1, :packed]])
    hs = reduce_all(pieces, owners)
    down_specs, down_args = [own(2, share, 0)], [expert_weights]
    for got in others:
        down_specs.append(other(share, 0))
        down_args.append(got[2])

    out = pl.pallas_call(
        functools.partial(down_kernel, parts),
        out_shape=jax.ShapeDtypeStruct((parts, rows, local), F32),
        grid_spec=pltpu.PrefetchScalarGridSpec(
            num_scalar_prefetch=4,
            grid=(experts,),
            in_specs=[line, line, *[whole(packed, cols)] * HALVES] + down_specs,
            out_specs=whole(parts, rows, local),
        ),
        compiler_params=params,
        cost_estimate=pl.CostEstimate(flops=2 * packed * local * parts * (share + 2 * rows), bytes_accessed=2 * 10**7, transcendentals=0),
    )(*scalars, slots, gates, *hs, *down_args)

    total = lax.dynamic_index_in_dim(out, 0, 0, keepdims=False)
    for s in range(1, parts):
        total = total + lax.ppermute(out[s], "fsdp", [(i, (i - s) % parts) for i in range(parts)])
    y = total.astype(BF16).reshape(steps, owners, block_rows, local)
    y = lax.all_to_all(y, "expert", split_axis=1, concat_axis=1, tiled=True)
    return jnp.transpose(y, (0, 2, 1, 3)).reshape(steps, block_rows, owners * local)


def solution(mesh):
    return jax.shard_map(
        body,
        mesh=mesh,
        in_specs=(
            P(None, "expert", None),
            P(None, "expert", None),
            P(None, "expert", None),
            P(),
            P(),
            P(None, ("fsdp", "expert"), None),
        ),
        out_specs=P(None, "expert", "fsdp"),
        check_vma=False,
    )
```

```python
import functools

import jax
import jax.numpy as jnp
from jax import lax
from jax.experimental import pallas as pl
from jax.experimental.pallas import tpu as pltpu
from jax.sharding import PartitionSpec as P

TILE = 256
HALVES = 2
ALIGN = 16
BF16 = jnp.bfloat16
F32 = jnp.float32


def dot(a, b, ca=1, cb=0):
    return lax.dot_general(a, b, (((ca,), (cb,)), ((), ())), preferred_element_type=F32)


def tables(route_ids, gate_values, cap_limit, block_rows):
    rows = route_ids.shape[0]
    experts = cap_limit.shape[0]
    hot = route_ids[:, :, None] == jnp.arange(experts, dtype=jnp.int32)[None, None, :]
    chosen = jnp.any(hot, axis=1)
    gates = jnp.sum(jnp.where(hot, gate_values[:, :, None].astype(F32), 0.0), axis=1)
    at = jnp.arange(rows, dtype=jnp.int32)
    earlier = at[None, :] < at[:, None]
    same = at[None, :] // block_rows == at[:, None] // block_rows
    position = dot((earlier & same).astype(BF16), chosen.astype(BF16)).astype(jnp.int32)
    kept = chosen & (position < cap_limit[None, :])
    before = dot(earlier.astype(BF16), kept.astype(BF16)).astype(jnp.int32)
    counts = jnp.sum(kept.astype(jnp.int32), axis=0)
    padded = (counts + (ALIGN - 1)) // ALIGN * ALIGN
    es = jnp.arange(experts, dtype=jnp.int32)
    starts = jnp.sum(jnp.where(es[None, :] < es[:, None], padded[None, :], 0), axis=1)
    slots = jnp.where(kept, before + starts[None, :], -1)
    chunks = (counts + (TILE - 1)) // TILE
    return slots.T[:, None, :], gates.T[:, None, :], starts, chunks


def up_kernel(parts, fresh, starts, chunks, order, mine, *refs):
    if fresh:
        slots_ref, x_ref, weights, (out_ref, packed_ref) = refs[0], refs[1], refs[2:-2], refs[-2:]
    else:
        packed_ref, weights, out_ref = refs[0], refs[1:-1], refs[-1]
    e = pl.program_id(0)

    @pl.when(e == 0)
    def _():
        out_ref[...] = jnp.zeros_like(out_ref)

    def step(c, carry):
        base = pl.multiple_of(starts[e] + c * TILE, ALIGN)
        if fresh:
            slots = slots_ref[0]
            pick = slots == base + lax.broadcasted_iota(jnp.int32, (TILE, slots.shape[1]), 0)
            pick = pick.astype(F32).astype(BF16)
        a = b = None
        for i in range(parts):
            if fresh:
                xs = dot(pick, x_ref[i]).astype(BF16)
                packed_ref[i, pl.ds(base, TILE), :] = xs
            else:
                xs = packed_ref[i, pl.ds(base, TILE), :]
            da = dot(xs, weights[2 * i][0])
            db = dot(xs, weights[2 * i + 1][0])
            a, b = (da, db) if a is None else (a + da, b + db)
        out_ref[0, pl.ds(base, TILE), :] = a.astype(out_ref.dtype)
        out_ref[1, pl.ds(base, TILE), :] = b.astype(out_ref.dtype)
        return carry

    lax.fori_loop(0, chunks[e], step, 0)


def down_kernel(parts, starts, chunks, order, mine, slots_ref, gates_ref, *refs):
    h_refs, weights, out_ref = refs[: 2 * HALVES], refs[2 * HALVES : -1], refs[-1]
    e = pl.program_id(0)
    total = h_refs[0].shape[0]

    @pl.when(e == 0)
    def _():
        out_ref[...] = jnp.zeros_like(out_ref)

    slots = slots_ref[0]
    gates = gates_ref[0]

    def step(c, carry):
        first = starts[e] + c * TILE
        base = pl.multiple_of(jnp.minimum(first, total - TILE), ALIGN)
        number = base + lax.broadcasted_iota(jnp.int32, (TILE, slots.shape[1]), 0)
        mix = jnp.where((slots == number) & (number >= first), gates, 0.0).astype(BF16)
        h = jnp.concatenate([h_ref[pl.ds(base, TILE), :] for h_ref in h_refs], axis=1)
        mix = jnp.concatenate([mix, mix], axis=0)
        for i in range(parts):
            y = dot(h, weights[i][0], 1, 1)
            high = y.astype(BF16)
            low = (y - high.astype(F32)).astype(BF16)
            out_ref[i] += dot(mix, jnp.concatenate([high, low], axis=0), 0, 0)
        return carry

    lax.fori_loop(0, chunks[e], step, 0)


def halve(cur, left, b, n):
    axis = left.index(b)
    bit = (lax.axis_index("expert") >> b) & 1
    send = lax.dynamic_index_in_dim(cur, 1 - bit, axis, keepdims=False).astype(BF16)
    keep = lax.dynamic_index_in_dim(cur, bit, axis, keepdims=False).astype(F32)
    got = lax.ppermute(send, "expert", [(i, i ^ (1 << b)) for i in range(n)])
    return keep + got.astype(F32), [i for i in left if i != b]


def double(cur, have, b, n):
    axis = sum(i > b for i in have)
    first = ((lax.axis_index("expert") >> b) & 1) == 0
    got = lax.ppermute(cur, "expert", [(i, i ^ (1 << b)) for i in range(n)])
    low, high = jnp.where(first, cur, got), jnp.where(first, got, cur)
    return jnp.stack([low, high], axis), sorted(have + [b], reverse=True)


def exchange_all(pieces, n):
    bits = n.bit_length() - 1
    later = list(range(2, bits))
    orders = ([0, 1] + later, [1, 0] + later)
    left = list(range(bits - 1, -1, -1))
    state = [[(i.reshape((2,) * bits + (i.shape[0] // n, i.shape[1])), left) for i in pair] for pair in pieces]
    for turn in range(2 * bits + 2 * (len(state) - 1)):
        for q in range(len(state)):
            at = turn - 2 * q
            if 0 <= at < bits:
                state[q] = [halve(*state[q][k], orders[k][at], n) for k in range(2)]
            if at == bits - 1:
                a, b = (i for i, _ in state[q])
                h = (a * jax.nn.sigmoid(a) * b).astype(BF16)
                cols = h.shape[1] // 2
                state[q] = [(h[:, :cols], []), (h[:, cols:], [])]
            if bits <= at < 2 * bits:
                state[q] = [double(*state[q][k], orders[k][2 * bits - 1 - at], n) for k in range(2)]
        held = lax.optimization_barrier([[i for i, _ in pair] for pair in state])
        state = [[(i, pair[k][1]) for k, i in enumerate(new)] for new, pair in zip(held, state)]
    return [i.reshape(-1, i.shape[-1]) for pair in state for i, _ in pair]


def body(tokens, route_ids, gate_values, cap_limit, update_ids, expert_weights):
    steps, block_rows, width = tokens.shape
    top = route_ids.shape[2]
    experts = cap_limit.shape[0]
    parts = lax.axis_size("fsdp")
    owners = lax.axis_size("expert")
    local = expert_weights.shape[1]
    hidden = expert_weights.shape[2] // 3
    share = hidden // parts
    rows = steps * owners * block_rows
    f = lax.axis_index("fsdp")

    es = jnp.arange(experts, dtype=jnp.int32)
    order = jnp.sum(jnp.where(update_ids[None, :] == es[:, None], es[None, :], 0), axis=1)

    others = []
    for s in range(1, parts):
        to = (f + s) % parts
        pairs = [(i, (i + s) % parts) for i in range(parts)]
        cuts = [
            lax.dynamic_slice(expert_weights, (0, 0, kind * hidden + to * share), (experts, local, share))
            for kind in range(3)
        ]
        others.append([lax.ppermute(cut, "fsdp", pairs) for cut in cuts])

    x = tokens.reshape(steps, block_rows, parts, owners, local)
    x = jnp.transpose(x, (3, 0, 1, 2, 4)).reshape(owners, steps, block_rows, parts * local)
    routes = jnp.concatenate([route_ids.astype(BF16), gate_values], axis=2)
    routes = jnp.broadcast_to(routes[None], (owners,) + routes.shape)
    x = jnp.concatenate([x, routes], axis=3)
    x = lax.all_to_all(x, "expert", split_axis=0, concat_axis=0, tiled=True)
    x = jnp.transpose(x, (1, 0, 2, 3)).reshape(rows, parts * local + 2 * top)
    ids = x[:, parts * local : parts * local + top].astype(jnp.int32)
    gate = x[:, parts * local + top :]
    slots, gates, starts, chunks = tables(ids, gate, cap_limit, block_rows)
    sources = [(f - s) % parts for s in range(parts)]
    x = jnp.stack([lax.dynamic_slice(x, (0, i * local), (rows, local)) for i in sources])

    packed = -(-(rows * top + experts * (ALIGN - 1)) // (ALIGN * owners)) * ALIGN * owners
    mine = f.astype(jnp.int32).reshape(1)
    whole = lambda *shape: pl.BlockSpec(shape, lambda e, *_: (0,) * len(shape))
    line = pl.BlockSpec((1, 1, rows), lambda e, *_: (e, 0, 0))

    def own(kind, cols, q):
        return pl.BlockSpec((1, local, cols), lambda e, st, ch, od, mi: (od[e], 0, (kind * parts + mi[0]) * (share // cols) + q))

    def other(cols, q):
        return pl.BlockSpec((1, local, cols), lambda e, st, ch, od, mi: (od[e], 0, q))

    scalars = (starts, chunks, order, mine)
    params = pltpu.CompilerParams(vmem_limit_bytes=58 * 2**20)
    cols = share // HALVES
    xs = None
    pieces = []
    for q in range(HALVES):
        specs, args = [own(0, cols, q), own(1, cols, q)], [expert_weights] * 2
        for got in others:
            specs += [other(cols, q)] * 2
            args += got[:2]
        ab_shape = (2, packed + TILE, cols)
        xs_shape = (parts, packed + TILE, local)
        fresh = q == 0
        made = pl.pallas_call(
            functools.partial(up_kernel, parts, fresh),
            out_shape=[jax.ShapeDtypeStruct(i, BF16) for i in ([ab_shape, xs_shape] if fresh else [ab_shape])],
            grid_spec=pltpu.PrefetchScalarGridSpec(
                num_scalar_prefetch=4,
                grid=(experts,),
                in_specs=([line, whole(parts, rows, local)] if fresh else [whole(*xs_shape)]) + specs,
                out_specs=[whole(*i) for i in ([ab_shape, xs_shape] if fresh else [ab_shape])],
            ),
            compiler_params=params,
            cost_estimate=pl.CostEstimate(flops=2 * 10**10, bytes_accessed=5 * 10**7, transcendentals=0),
        )(*scalars, *([slots, x] if fresh else [xs]), *args)
        if fresh:
            xs = made[1]
        ab = made[0]
        pieces.append([ab[0, :packed], ab[1, :packed]])
    hs = exchange_all(pieces, owners)
    down_specs, down_args = [own(2, share, 0)], [expert_weights]
    for got in others:
        down_specs.append(other(share, 0))
        down_args.append(got[2])

    out = pl.pallas_call(
        functools.partial(down_kernel, parts),
        out_shape=jax.ShapeDtypeStruct((parts, rows, local), F32),
        grid_spec=pltpu.PrefetchScalarGridSpec(
            num_scalar_prefetch=4,
            grid=(experts,),
            in_specs=[line, line, *[whole(packed, cols // 2)] * (2 * HALVES)] + down_specs,
            out_specs=whole(parts, rows, local),
        ),
        compiler_params=params,
        cost_estimate=pl.CostEstimate(flops=2 * packed * local * parts * (share + 2 * rows), bytes_accessed=2 * 10**7, transcendentals=0),
    )(*scalars, slots, gates, *hs, *down_args)

    total = lax.dynamic_index_in_dim(out, 0, 0, keepdims=False)
    for s in range(1, parts):
        total = total + lax.ppermute(out[s], "fsdp", [(i, (i - s) % parts) for i in range(parts)])
    y = total.astype(BF16).reshape(steps, owners, block_rows, local)
    y = lax.all_to_all(y, "expert", split_axis=1, concat_axis=1, tiled=True)
    return jnp.transpose(y, (0, 2, 1, 3)).reshape(steps, block_rows, owners * local)


def solution(mesh):
    return jax.shard_map(
        body,
        mesh=mesh,
        in_specs=(
            P(None, "expert", None),
            P(None, "expert", None),
            P(None, "expert", None),
            P(),
            P(),
            P(None, ("fsdp", "expert"), None),
        ),
        out_specs=P(None, "expert", "fsdp"),
        check_vma=False,
    )
```

```python
import functools

import jax
import jax.numpy as jnp
from jax import lax
from jax.experimental import pallas as pl
from jax.experimental.pallas import tpu as pltpu
from jax.sharding import PartitionSpec as P

TILE = 256
HALVES = 2
ALIGN = 16
BF16 = jnp.bfloat16
F32 = jnp.float32


def dot(a, b, ca=1, cb=0):
    return lax.dot_general(a, b, (((ca,), (cb,)), ((), ())), preferred_element_type=F32)


def tables(route_ids, gate_values, cap_limit, block_rows):
    rows = route_ids.shape[0]
    experts = cap_limit.shape[0]
    hot = route_ids[:, :, None] == jnp.arange(experts, dtype=jnp.int32)[None, None, :]
    chosen = jnp.any(hot, axis=1)
    gates = jnp.sum(jnp.where(hot, gate_values[:, :, None].astype(F32), 0.0), axis=1)
    at = jnp.arange(rows, dtype=jnp.int32)
    earlier = at[None, :] < at[:, None]
    same = at[None, :] // block_rows == at[:, None] // block_rows
    position = dot((earlier & same).astype(BF16), chosen.astype(BF16)).astype(jnp.int32)
    kept = chosen & (position < cap_limit[None, :])
    before = dot(earlier.astype(BF16), kept.astype(BF16)).astype(jnp.int32)
    counts = jnp.sum(kept.astype(jnp.int32), axis=0)
    padded = (counts + (ALIGN - 1)) // ALIGN * ALIGN
    es = jnp.arange(experts, dtype=jnp.int32)
    starts = jnp.sum(jnp.where(es[None, :] < es[:, None], padded[None, :], 0), axis=1)
    slots = jnp.where(kept, before + starts[None, :], -1)
    chunks = (counts + (TILE - 1)) // TILE
    return slots.T[:, None, :], gates.T[:, None, :], starts, chunks


def up_kernel(parts, fresh, starts, chunks, order, mine, *refs):
    if fresh:
        slots_ref, x_ref, weights, (a_ref, b_ref, packed_ref) = refs[0], refs[1], refs[2:-3], refs[-3:]
    else:
        packed_ref, weights, (a_ref, b_ref) = refs[0], refs[1:-2], refs[-2:]
    e = pl.program_id(0)
    total = a_ref.shape[0]

    @pl.when(e == 0)
    def _():
        a_ref[...] = jnp.zeros_like(a_ref)
        b_ref[...] = jnp.zeros_like(b_ref)

    def step(c, carry):
        first = starts[e] + c * TILE
        base = pl.multiple_of(jnp.minimum(first, total - TILE), ALIGN)
        ours = pl.ds(base, TILE)
        fits = (base + lax.broadcasted_iota(jnp.int32, (TILE, 1), 0)) >= first
        if fresh:
            slots = slots_ref[0]
            pick = slots == base + lax.broadcasted_iota(jnp.int32, (TILE, slots.shape[1]), 0)
            pick = pick.astype(F32).astype(BF16)
        a = b = None
        for i in range(parts):
            if fresh:
                xs = dot(pick, x_ref[i])
                xs = jnp.where(fits, xs, packed_ref[i, ours, :].astype(F32)).astype(BF16)
                packed_ref[i, ours, :] = xs
            else:
                xs = packed_ref[i, ours, :]
            da = dot(xs, weights[2 * i][0])
            db = dot(xs, weights[2 * i + 1][0])
            a, b = (da, db) if a is None else (a + da, b + db)
        a_ref[ours, :] = jnp.where(fits, a, a_ref[ours, :].astype(F32)).astype(BF16)
        b_ref[ours, :] = jnp.where(fits, b, b_ref[ours, :].astype(F32)).astype(BF16)
        return carry

    lax.fori_loop(0, chunks[e], step, 0)


def down_kernel(parts, starts, chunks, order, mine, slots_ref, gates_ref, *refs):
    h_refs, weights, out_ref = refs[: 2 * HALVES], refs[2 * HALVES : -1], refs[-1]
    e = pl.program_id(0)
    total = h_refs[0].shape[0]

    @pl.when(e == 0)
    def _():
        out_ref[...] = jnp.zeros_like(out_ref)

    slots = slots_ref[0]
    gates = gates_ref[0]

    def step(c, carry):
        first = starts[e] + c * TILE
        base = pl.multiple_of(jnp.minimum(first, total - TILE), ALIGN)
        number = base + lax.broadcasted_iota(jnp.int32, (TILE, slots.shape[1]), 0)
        mix = jnp.where((slots == number) & (number >= first), gates, 0.0).astype(BF16)
        h = jnp.concatenate([h_ref[pl.ds(base, TILE), :] for h_ref in h_refs], axis=1)
        mix = jnp.concatenate([mix, mix], axis=0)
        for i in range(parts):
            y = dot(h, weights[i][0], 1, 1)
            high = y.astype(BF16)
            low = (y - high.astype(F32)).astype(BF16)
            out_ref[i] += dot(mix, jnp.concatenate([high, low], axis=0), 0, 0)
        return carry

    lax.fori_loop(0, chunks[e], step, 0)


def halve(cur, left, b, n):
    axis = left.index(b)
    bit = (lax.axis_index("expert") >> b) & 1
    low, high = (lax.index_in_dim(cur, i, axis, keepdims=False) for i in range(2))
    send = jnp.where(bit == 1, low, high).astype(BF16)
    keep = jnp.where(bit == 1, high, low).astype(F32)
    got = lax.ppermute(send, "expert", [(i, i ^ (1 << b)) for i in range(n)])
    return keep + got.astype(F32), [i for i in left if i != b]


def double(cur, have, b, n):
    axis = sum(i > b for i in have)
    first = ((lax.axis_index("expert") >> b) & 1) == 0
    got = lax.ppermute(cur, "expert", [(i, i ^ (1 << b)) for i in range(n)])
    low, high = jnp.where(first, cur, got), jnp.where(first, got, cur)
    return jnp.stack([low, high], axis), sorted(have + [b], reverse=True)


def exchange_all(pieces, n):
    bits = n.bit_length() - 1
    later = list(range(2, bits))
    orders = ([0, 1] + later, [1, 0] + later)
    left = list(range(bits - 1, -1, -1))
    state = [[(i.reshape((2,) * bits + (i.shape[0] // n, i.shape[1])), left) for i in pair] for pair in pieces]
    for turn in range(2 * bits + 2 * (len(state) - 1)):
        for q in range(len(state)):
            at = turn - 2 * q
            if 0 <= at < bits:
                state[q] = [halve(*state[q][k], orders[k][at], n) for k in range(2)]
            if at == bits - 1:
                a, b = (i for i, _ in state[q])
                h = (a * jax.nn.sigmoid(a) * b).astype(BF16)
                cols = h.shape[1] // 2
                state[q] = [(h[:, :cols], []), (h[:, cols:], [])]
            if bits <= at < 2 * bits:
                state[q] = [double(*state[q][k], orders[k][2 * bits - 1 - at], n) for k in range(2)]
        held = lax.optimization_barrier([[i for i, _ in pair] for pair in state])
        state = [[(i, pair[k][1]) for k, i in enumerate(new)] for new, pair in zip(held, state)]
    return [i.reshape(-1, i.shape[-1]) for pair in state for i, _ in pair]


def body(tokens, route_ids, gate_values, cap_limit, update_ids, expert_weights):
    steps, block_rows, width = tokens.shape
    top = route_ids.shape[2]
    experts = cap_limit.shape[0]
    parts = lax.axis_size("fsdp")
    owners = lax.axis_size("expert")
    local = expert_weights.shape[1]
    hidden = expert_weights.shape[2] // 3
    share = hidden // parts
    rows = steps * owners * block_rows
    f = lax.axis_index("fsdp")

    es = jnp.arange(experts, dtype=jnp.int32)
    order = jnp.sum(jnp.where(update_ids[None, :] == es[:, None], es[None, :], 0), axis=1)

    others = []
    for s in range(1, parts):
        to = (f + s) % parts
        pairs = [(i, (i + s) % parts) for i in range(parts)]
        cuts = [
            lax.dynamic_slice(expert_weights, (0, 0, kind * hidden + to * share), (experts, local, share))
            for kind in range(3)
        ]
        others.append([lax.ppermute(cut, "fsdp", pairs) for cut in cuts])

    x = tokens.reshape(steps, block_rows, parts, owners, local)
    x = jnp.transpose(x, (3, 0, 1, 2, 4)).reshape(owners, steps, block_rows, parts * local)
    routes = jnp.concatenate([route_ids.astype(BF16), gate_values], axis=2)
    routes = jnp.broadcast_to(routes[None], (owners,) + routes.shape)
    x = jnp.concatenate([x, routes], axis=3)
    x = lax.all_to_all(x, "expert", split_axis=0, concat_axis=0, tiled=True)
    x = jnp.transpose(x, (1, 0, 2, 3)).reshape(rows, parts * local + 2 * top)
    ids = x[:, parts * local : parts * local + top].astype(jnp.int32)
    gate = x[:, parts * local + top :]
    slots, gates, starts, chunks = tables(ids, gate, cap_limit, block_rows)
    sources = [(f - s) % parts for s in range(parts)]
    x = jnp.stack([lax.dynamic_slice(x, (0, i * local), (rows, local)) for i in sources])

    packed = -(-(rows * top + experts * (ALIGN - 1)) // (ALIGN * owners)) * ALIGN * owners
    mine = f.astype(jnp.int32).reshape(1)
    whole = lambda *shape: pl.BlockSpec(shape, lambda e, *_: (0,) * len(shape))
    line = pl.BlockSpec((1, 1, rows), lambda e, *_: (e, 0, 0))

    def own(kind, cols, q):
        return pl.BlockSpec((1, local, cols), lambda e, st, ch, od, mi: (od[e], 0, (kind * parts + mi[0]) * (share // cols) + q))

    def other(cols, q):
        return pl.BlockSpec((1, local, cols), lambda e, st, ch, od, mi: (od[e], 0, q))

    scalars = (starts, chunks, order, mine)
    params = pltpu.CompilerParams(vmem_limit_bytes=58 * 2**20)
    cols = share // HALVES
    xs = None
    pieces = []
    for q in range(HALVES):
        specs, args = [own(0, cols, q), own(1, cols, q)], [expert_weights] * 2
        for got in others:
            specs += [other(cols, q)] * 2
            args += got[:2]
        ab_shape = (packed, cols)
        xs_shape = (parts, packed, local)
        fresh = q == 0
        made = pl.pallas_call(
            functools.partial(up_kernel, parts, fresh),
            out_shape=[jax.ShapeDtypeStruct(i, BF16) for i in ([ab_shape] * 2 + [xs_shape] * fresh)],
            grid_spec=pltpu.PrefetchScalarGridSpec(
                num_scalar_prefetch=4,
                grid=(experts,),
                in_specs=([line, whole(parts, rows, local)] if fresh else [whole(*xs_shape)]) + specs,
                out_specs=[whole(*i) for i in ([ab_shape] * 2 + [xs_shape] * fresh)],
            ),
            compiler_params=params,
            cost_estimate=pl.CostEstimate(flops=2 * 10**10, bytes_accessed=5 * 10**7, transcendentals=0),
        )(*scalars, *([slots, x] if fresh else [xs]), *args)
        if fresh:
            xs = made[2]
        pieces.append(made[:2])
    hs = exchange_all(pieces, owners)
    down_specs, down_args = [own(2, share, 0)], [expert_weights]
    for got in others:
        down_specs.append(other(share, 0))
        down_args.append(got[2])

    out = pl.pallas_call(
        functools.partial(down_kernel, parts),
        out_shape=jax.ShapeDtypeStruct((parts, rows, local), F32),
        grid_spec=pltpu.PrefetchScalarGridSpec(
            num_scalar_prefetch=4,
            grid=(experts,),
            in_specs=[line, line, *[whole(packed, cols // 2)] * (2 * HALVES)] + down_specs,
            out_specs=whole(parts, rows, local),
        ),
        compiler_params=params,
        cost_estimate=pl.CostEstimate(flops=2 * packed * local * parts * (share + 2 * rows), bytes_accessed=2 * 10**7, transcendentals=0),
    )(*scalars, slots, gates, *hs, *down_args)

    total = lax.dynamic_index_in_dim(out, 0, 0, keepdims=False)
    for s in range(1, parts):
        total = total + lax.ppermute(out[s], "fsdp", [(i, (i - s) % parts) for i in range(parts)])
    y = total.astype(BF16).reshape(steps, owners, block_rows, local)
    y = lax.all_to_all(y, "expert", split_axis=1, concat_axis=1, tiled=True)
    return jnp.transpose(y, (0, 2, 1, 3)).reshape(steps, block_rows, owners * local)


def solution(mesh):
    return jax.shard_map(
        body,
        mesh=mesh,
        in_specs=(
            P(None, "expert", None),
            P(None, "expert", None),
            P(None, "expert", None),
            P(),
            P(),
            P(None, ("fsdp", "expert"), None),
        ),
        out_specs=P(None, "expert", "fsdp"),
        check_vma=False,
    )
```
